256 devices in a mesh: ctx: 32 (over z_lo, x, core), ch: 8 (over y, z_hi).
Axes of the slice: x: 4, y: 4, z: 8 (z_hi: 2, z_lo: 4; z = z_hi * 4 + z_lo), core: 2. Of those that a mesh axis runs over, the one named last changes fastest.
Arguments:
- activations: bfloat16 [4096, 4096], P('ctx', 'ch'), may hold values from -420 to 420
- norm_gain: float32 [4096], P('ch'), may hold values from 0.1 to 1.9
- filter_taps: bfloat16 [4096, 4096], P('ctx', 'ch'), may hold values from -2 to 2
- out_grad: bfloat16 [4096, 4096], P('ctx', 'ch'), may hold values from -6 to 6
- block_order: int32 [32], replicated, may hold values from 0 to 31, each once
- lag_order: int32 [32], replicated, may hold values from 0 to 31, each once
Outputs:
- mixed: bfloat16 [4096, 4096], P('ctx', 'ch')
- normed_grad: bfloat16 [4096, 4096], P('ctx', 'ch')
- taps_grad: float32 [4096, 4096], P('ctx', 'ch')
The draws below stay inside these ranges and needn't reach their ends.
Inputs may be any that keep to these rules, and one draw needn't show every extreme that they name: `block_order`: a permutation of the block numbers. `lag_order`: a permutation of the lag block numbers.
All inputs are finite; a program needn't handle non-finite values.
Results may differ from the reference program's by a relative error of at most 0.005.
Values may be sent and summed in bfloat16 or wider, within the bound.
No kernel may reach another device: no remote copies, remote signals or barrier semaphores. Data moves between devices by JAX's collectives and lax.ppermute only.
A program may use at most 192 MiB of HBM per device.

```python
import math
import jax
import jax.numpy as jnp
from jax import lax

BLK = 128
TOKENS = 4096
CH = 4096
N_CTX = 32


def draw_activations(key, part):
    key = jax.random.fold_in(key, 11)
    first, second, third = jax.random.split(key, 3)
    columns = jnp.arange(CH, dtype=jnp.float32) / CH
    col_scale = jnp.exp(jnp.log(3.0) * columns) * jnp.exp(jax.random.uniform(second, (CH,), minval=0.0, maxval=jnp.log(3.4)))
    base = jnp.clip(jax.random.normal(first, (TOKENS, CH)), -4.0, 4.0)
    row_scale = jnp.exp(jax.random.uniform(third, (TOKENS, 1), minval=0.0, maxval=jnp.log(10.0)))
    return (base * row_scale * col_scale[None, :]).astype(jnp.bfloat16)


def draw_filter_taps(key, part):
    key = jax.random.fold_in(key, 23)
    first, second, third, fourth = jax.random.split(key, 4)
    lags = jnp.arange(TOKENS, dtype=jnp.float32)[:, None]
    slow_share = 0.5
    rough = jnp.clip(jax.random.normal(first, (TOKENS, CH)), -4.0, 4.0)
    slow = jax.random.uniform(second, (1, CH)) < slow_share
    slow_rate = jax.random.uniform(third, (1, CH), minval=0.1, maxval=2.0) / TOKENS
    fast_rate = jnp.exp(jax.random.uniform(fourth, (1, CH), minval=jnp.log(1.0 / 50.0), maxval=jnp.log(1.0 / 10.0)))
    rate = jnp.where(slow, slow_rate, fast_rate)
    amplitude = jnp.sqrt((1.0 - jnp.exp(-2.0 * rate)) / (1.0 - jnp.exp(-2.0 * rate * TOKENS)))
    return (rough * amplitude * jnp.exp(-rate * lags)).astype(jnp.bfloat16)


def steps_of(key, shape, cuts, low, high):
    def one(axis_at, parts):
        steps = jax.random.uniform(jax.random.fold_in(jax.random.fold_in(key, 6), axis_at), (parts,), jnp.float32, low / len(cuts), high / len(cuts))
        return jnp.repeat(jnp.exp(steps), shape[axis_at] // parts).reshape((-1,) + (1,) * (len(shape) - axis_at - 1))

    factor_of = one(*cuts[0])
    for cut in cuts[1:]:
        factor_of = factor_of * one(*cut)
    return factor_of


def normal_values(own_key, shape, width, reach, shards=(), held_as=jnp.bfloat16):
    values = width * jax.random.normal(own_key, shape, jnp.float32)
    if shards:
        values = values * steps_of(own_key, shape, shards, -0.22, 0.18)
    return jnp.clip(values, -reach, reach).astype(held_as)


def setup_inputs(seed: int = 0) -> dict:
    key_of = jax.random.split(jax.random.key(seed), 7)
    return {
        "activations": draw_activations(jax.random.fold_in(key_of[6], 71), 0),
        "norm_gain": jnp.clip(1.0 + 0.18 * jax.random.normal(key_of[1], (CH,), jnp.float32), 0.1, 1.9),
        "filter_taps": draw_filter_taps(jax.random.fold_in(key_of[6], 71), 0),
        "out_grad": normal_values(key_of[3], (TOKENS, CH), 1.0, 6.0, ((0, 32), (1, 8))),
        "block_order": jax.random.permutation(key_of[4], N_CTX).astype(jnp.int32),
        "lag_order": jax.random.permutation(key_of[5], N_CTX).astype(jnp.int32),
    }


EPS = 1e-06

def to_sequence(tensor, ordering):
    pieces = tensor.reshape(N_CTX, BLK, tensor.shape[1])
    placed = jnp.zeros_like(pieces).at[ordering].set(pieces)
    return placed.reshape(TOKENS, tensor.shape[1])

def to_devices(tensor, ordering):
    pieces = tensor.reshape(N_CTX, BLK, tensor.shape[1])
    return pieces[ordering].reshape(TOKENS, tensor.shape[1])

def causal_conv(filters, signal):
    length = 2 * TOKENS
    spectra = jnp.fft.rfft(filters, n=length, axis=0) * jnp.fft.rfft(signal, n=length, axis=0)
    return jnp.fft.irfft(spectra, n=length, axis=0)[:TOKENS]

def causal_corr(kernel, signal):
    length = 2 * TOKENS
    spectra = jnp.conj(jnp.fft.rfft(kernel, n=length, axis=0)) * jnp.fft.rfft(signal, n=length, axis=0)
    return jnp.fft.irfft(spectra, n=length, axis=0)[:TOKENS]

def reference(activations, norm_gain, filter_taps, out_grad, block_order, lag_order):
    values = activations.astype(jnp.float32)
    inv_norm = lax.rsqrt(lax.optimization_barrier(jnp.sum(values * values, axis=1, keepdims=True)) / CH + EPS)
    normed = (values * inv_norm * norm_gain[None, :]).astype(jnp.bfloat16)
    signal = to_sequence(normed.astype(jnp.float32), block_order)
    filters = to_sequence(filter_taps.astype(jnp.float32), lag_order)
    grads = to_sequence(out_grad.astype(jnp.float32), block_order)
    mixed = to_devices(causal_conv(filters, signal), block_order).astype(jnp.bfloat16)
    normed_grad = to_devices(causal_corr(filters, grads), block_order).astype(jnp.bfloat16)
    taps_grad = to_devices(causal_corr(signal, grads), lag_order) * (1.0 / math.sqrt(TOKENS))
    return (mixed, normed_grad, taps_grad)
```

```python
import functools
import math

import jax
import jax.numpy as jnp
import ml_dtypes
import numpy as np
from jax import lax
from jax.experimental import pallas as pl
from jax.experimental.pallas import tpu as pltpu
from jax.sharding import PartitionSpec as P

EPS = 1e-06
BLOCKS = 32
BLK = 128
LANES = 16
POINTS = BLOCKS * BLK
ROWS = BLOCKS * LANES
SLOW = 4
FAST = BLOCKS // SLOW
BF16 = jnp.bfloat16
F32 = jnp.float32


def halves(matrix):
    high = matrix.astype(np.float32).astype(ml_dtypes.bfloat16)
    low = (matrix - high.astype(np.float64)).astype(np.float32).astype(ml_dtypes.bfloat16)
    return np.concatenate([high, high, low], axis=0)


@functools.lru_cache(maxsize=1)
def tables():
    block = np.arange(BLOCKS)
    spot = np.arange(BLK)
    turn = np.exp(-2j * np.pi * np.outer(block + 0.25, spot) / POINTS)
    inner = np.exp(-2j * np.pi * np.outer(spot, spot) / BLK)
    forth = np.block([[inner.real, inner.imag], [-inner.imag, inner.real]])
    home = np.block([[inner.real, -inner.imag], [inner.imag, inner.real]]) / POINTS
    turns = np.stack([turn.real, turn.imag]).astype(np.float32)
    return turns, halves(forth), halves(home)


def plus(a, b):
    return a[0] + b[0], a[1] + b[1]


def minus(a, b):
    return a[0] - b[0], a[1] - b[1]


def times_i(a, sign):
    return (-a[1], a[0]) if sign > 0 else (a[1], -a[0])


def times(a, b):
    return a[0] * b[0] - a[1] * b[1], a[0] * b[1] + a[1] * b[0]


def rotated(a, angle):
    if angle == 0.0:
        return a
    return times(a, (math.cos(angle), math.sin(angle)))


def four(z, sign):
    even, odd = plus(z[0], z[2]), minus(z[0], z[2])
    both, turn = plus(z[1], z[3]), times_i(minus(z[1], z[3]), sign)
    return [plus(even, both), plus(odd, turn), minus(even, both), minus(odd, turn)]


def eight(z, sign):
    even, odd = four(z[0::2], sign), four(z[1::2], sign)
    root = math.sqrt(0.5)
    a, b, c, d = odd
    first = ((b[0] - sign * b[1]) * root, (b[1] + sign * b[0]) * root)
    third = ((-d[0] - sign * d[1]) * root, (sign * d[0] - d[1]) * root)
    odd = [a, first, times_i(c, sign), third]
    return [plus(e, o) for e, o in zip(even, odd)] + [minus(e, o) for e, o in zip(even, odd)]


def store_split(ref, base, at, value):
    for part in range(2):
        high = value[part].astype(BF16)
        low = (value[part] - high.astype(F32)).astype(BF16)
        ref[pl.ds(base + at * LANES, LANES), pl.ds(part * BLK, BLK)] = high
        ref[pl.ds(base + at * LANES, LANES), pl.ds((2 + part) * BLK, BLK)] = low


def load_pair(ref, base, at):
    rows = pl.ds(base + at * LANES, LANES)
    return ref[rows, pl.ds(0, BLK)], ref[rows, pl.ds(BLK, BLK)]


def forward_blocks(load, turn_ref, mid_ref, lhs_ref, base):
    for b in range(FAST):
        x = [load(b + FAST * a) for a in range(SLOW)]
        z = [(x[0], jnp.zeros_like(x[0]))]
        for a in range(1, SLOW):
            angle = -math.pi * a / 8
            z.append((x[a] * math.cos(angle), x[a] * math.sin(angle)))
        for p, value in enumerate(four(z, -1)):
            value = rotated(value, -2 * math.pi * b * (p + 0.25) / BLOCKS)
            mid_ref[b * SLOW + p, 0] = value[0]
            mid_ref[b * SLOW + p, 1] = value[1]
        yield
    for p in range(SLOW):
        z = [(mid_ref[b * SLOW + p, 0], mid_ref[b * SLOW + p, 1]) for b in range(FAST)]
        for q, value in enumerate(eight(z, -1)):
            k = p + SLOW * q
            value = times(value, (turn_ref[0, pl.ds(k, 1), :], turn_ref[1, pl.ds(k, 1), :]))
            store_split(lhs_ref, base, k, value)
        yield


def backward_blocks(store, turn_ref, mid_ref, wave_ref, base):
    for p in range(SLOW):
        z = []
        for q in range(FAST):
            k = p + SLOW * q
            turn = (turn_ref[0, pl.ds(k, 1), :], -turn_ref[1, pl.ds(k, 1), :])
            z.append(times(load_pair(wave_ref, base, k), turn))
        for b, value in enumerate(eight(z, 1)):
            value = rotated(value, 2 * math.pi * b * (p + 0.25) / BLOCKS)
            mid_ref[b * SLOW + p, 0] = value[0]
            mid_ref[b * SLOW + p, 1] = value[1]
        yield
    for b in range(FAST):
        z = [(mid_ref[b * SLOW + p, 0], mid_ref[b * SLOW + p, 1]) for p in range(SLOW)]
        for a, value in enumerate(four(z, 1)):
            angle = math.pi * a / 8
            real = value[0] if a == 0 else value[0] * math.cos(angle) - value[1] * math.sin(angle)
            store(b + FAST * a, real)
        yield


def lane_step(source, table, target, base):
    part = ROWS // SLOW
    for at in range(SLOW):
        rows = pl.ds(base + at * part, part)
        left = jnp.concatenate([source[rows, :], source[rows, pl.ds(0, 2 * BLK)]], axis=1)
        target[rows, :] = jnp.dot(left, table[...], preferred_element_type=F32)
        yield


def together(*pieces):
    total = max(count for _, count in pieces)
    done = [0] * len(pieces)
    for turn in range(1, total + 1):
        for i, (step, count) in enumerate(pieces):
            while done[i] * total < turn * count:
                next(step)
                done[i] += 1
    for step, _ in pieces:
        next(step, None)


def slots_of(order_ref, slot_ref):
    for k in range(BLOCKS):
        slot_ref[order_ref[k]] = k


def prepare_kernel(
    x_hbm, gain_hbm, taps_hbm, grad_hbm, pair_ref, scaled_ref, x_ref, gain_ref, taps_ref, grad_ref, sems
):
    copies = [
        pltpu.make_async_copy(source, target, sems.at[i])
        for i, (source, target) in enumerate(
            ((taps_hbm, taps_ref), (grad_hbm, grad_ref), (x_hbm, x_ref), (gain_hbm, gain_ref))
        )
    ]
    for copy in copies:
        copy.start()
    copies[0].wait()
    taps = taps_ref[...].astype(F32).T.astype(BF16)
    pair_ref[:, :LANES, :] = taps.reshape(BLOCKS, LANES, BLK)
    copies[1].wait()
    grads = grad_ref[...].astype(F32).T.astype(BF16)
    pair_ref[:, LANES:, :] = grads.reshape(BLOCKS, LANES, BLK)
    copies[2].wait()
    copies[3].wait()
    scaled_ref[...] = (x_ref[...].astype(F32) * gain_ref[...]).T


def norm_kernel(width, scaled_ref, squares_ref, pair_ref, out_ref):
    inv_norm = lax.rsqrt(squares_ref[...] / width + EPS)
    normed = (scaled_ref[...] * inv_norm).astype(BF16)
    out_ref[:, : 2 * LANES, :] = pair_ref[...]
    out_ref[:, 2 * LANES :, :] = normed.reshape(BLOCKS, LANES, BLK)


def main_kernel(
    block_ref, lag_ref, all_ref, turn_ref, forth, home,
    out_ref,
    block_slot, lag_slot, mid_ref, lhs_ref, spec_ref, wave_ref,
):
    slots_of(block_ref, block_slot)
    slots_of(lag_ref, lag_slot)

    def load(slot, at):
        return lambda n: all_ref[slot[n], pl.ds(at * LANES, LANES), :].astype(F32)

    def store(slot, at):
        def one(n, value):
            out_ref[slot[n], pl.ds(at * LANES, LANES), :] = value.astype(BF16)

        return one

    loads = (load(lag_slot, 0), load(block_slot, 1), load(block_slot, 2))
    stores = (store(block_slot, 2), store(block_slot, 0), store(lag_slot, 1))

    def blocks_in(i):
        return forward_blocks(loads[i], turn_ref, mid_ref.at[i], lhs_ref, i * ROWS), FAST + SLOW

    def blocks_out(i):
        return backward_blocks(stores[i], turn_ref, mid_ref.at[i], wave_ref, i * ROWS), FAST + SLOW

    def lanes_in(i):
        return lane_step(lhs_ref, forth, spec_ref, i * ROWS), SLOW

    def lanes_out(i):
        return lane_step(lhs_ref, home, wave_ref, i * ROWS), SLOW

    def first_product():
        for k in range(BLOCKS):
            f, g = load_pair(spec_ref, 0, k), load_pair(spec_ref, ROWS, k)
            store_split(lhs_ref, 0, k, times((f[0], -f[1]), g))
            yield

    def other_products():
        for k in range(BLOCKS):
            f, g, s = (load_pair(spec_ref, i * ROWS, k) for i in range(3))
            store_split(lhs_ref, ROWS, k, times(f, s))
            store_split(lhs_ref, 2 * ROWS, k, times((s[0], -s[1]), g))
            yield

    together(blocks_in(0))
    together(lanes_in(0), blocks_in(1))
    together(lanes_in(1), blocks_in(2))
    together(lanes_in(2), (first_product(), BLOCKS))
    together(lanes_out(0), (other_products(), BLOCKS))
    together(lanes_out(1), blocks_out(0))
    together(lanes_out(2), blocks_out(1))
    together(blocks_out(2))


def finish_kernel(scale, in_ref, mixed_ref, grad_ref, taps_ref):
    channels = BLOCKS * LANES

    def flip(at):
        part = in_ref[:, at * LANES : (at + 1) * LANES, :]
        return part.astype(F32).reshape(channels, BLK).T

    mixed_ref[...] = flip(0).astype(BF16)
    taps_ref[...] = flip(1) * scale
    grad_ref[...] = flip(2).astype(BF16)


VMEM = pl.BlockSpec(memory_space=pltpu.VMEM)
SMEM = pl.BlockSpec(memory_space=pltpu.SMEM)
ANY = pl.BlockSpec(memory_space=pl.ANY)


def call(kernel, outs, specs, scratch=(), flops=0, moved=0):
    return pl.pallas_call(
        kernel,
        out_shape=outs,
        in_specs=specs,
        out_specs=jax.tree.map(lambda _: VMEM, outs),
        scratch_shapes=list(scratch),
        cost_estimate=pl.CostEstimate(flops=flops, bytes_accessed=moved, transcendentals=0),
        compiler_params=pltpu.CompilerParams(vmem_limit_bytes=24 * 2**20),
    )


def shaped(shape, dtype):
    return jax.ShapeDtypeStruct(shape, dtype)


def working():
    return [
        pltpu.SMEM((BLOCKS,), jnp.int32),
        pltpu.SMEM((BLOCKS,), jnp.int32),
        pltpu.VMEM((3, BLOCKS, 2, LANES, BLK), F32),
        pltpu.VMEM((3 * ROWS, 4 * BLK), BF16),
        pltpu.VMEM((3 * ROWS, 2 * BLK), F32),
        pltpu.VMEM((3 * ROWS, 2 * BLK), F32),
    ]


def per_device(activations, norm_gain, filter_taps, out_grad, block_order, lag_order):
    rows, channels = activations.shape
    width = channels * lax.axis_size("ch")
    exchange = functools.partial(
        lax.all_to_all, axis_name="ctx", split_axis=0, concat_axis=0, tiled=True
    )
    tile = pltpu.VMEM((rows, channels), BF16)
    values = activations.astype(F32)
    squares = jnp.sum(values * values, axis=1)
    pair, scaled = call(
        prepare_kernel,
        (
            shaped((BLOCKS, 2 * LANES, BLK), BF16),
            shaped((channels, rows), F32),
        ),
        [ANY] * 4,
        [tile, pltpu.VMEM((1, channels), F32), tile, tile, pltpu.SemaphoreType.DMA((4,))],
        moved=2**20,
    )(activations, norm_gain.reshape(1, channels), filter_taps, out_grad)

    for step in (1, 2, 6):
        hop = [(i, i ^ step) for i in range(8)]
        squares = squares + lax.ppermute(squares, "ch", hop)
        if step == 1:
            squares, pair, scaled = lax.optimization_barrier((squares, pair, scaled))
    normed = call(
        functools.partial(norm_kernel, width),
        shaped((BLOCKS, 3 * LANES, BLK), BF16),
        [VMEM] * 3,
        moved=2**19,
    )(scaled, squares.reshape(1, rows), pair)
    signal = exchange(normed)

    fixed = [jnp.asarray(t) for t in tables()]
    spec = shaped((ROWS, 2 * BLK), F32)
    out = call(
        main_kernel,
        shaped((BLOCKS, 3 * LANES, BLK), BF16),
        [SMEM] * 2 + [VMEM] * 4,
        working(),
        flops=2 * 10**9,
        moved=2 * 2**20,
    )(block_order, lag_order, signal, *fixed)
    out = exchange(out)
    return call(
        functools.partial(finish_kernel, 1.0 / math.sqrt(POINTS)),
        (
            shaped((rows, channels), BF16),
            shaped((rows, channels), BF16),
            shaped((rows, channels), F32),
        ),
        [VMEM],
        moved=2**20,
    )(out)


def solution(mesh):
    placed = (P("ctx", "ch"), P("ch"), P("ctx", "ch"), P("ctx", "ch"), P(), P())
    return jax.shard_map(
        per_device,
        mesh=mesh,
        in_specs=placed,
        out_specs=(P("ctx", "ch"), P("ctx", "ch"), P("ctx", "ch")),
        check_vma=False,
    )
```

```python
import functools
import math

import jax
import jax.numpy as jnp
import ml_dtypes
import numpy as np
from jax import lax
from jax.experimental import pallas as pl
from jax.experimental.pallas import tpu as pltpu
from jax.sharding import PartitionSpec as P

EPS = 1e-06
BLOCKS = 32
BLK = 128
LANES = 16
POINTS = BLOCKS * BLK
ROWS = BLOCKS * LANES
SLOW = 4
FAST = BLOCKS // SLOW
RANKS = [23, 22, 21, 20, 19, 18, 17, 16, 15, 14, 13, 12, 11, 10, 9, 8, 31, 30, 29, 28, 27, 26, 25, 24, 7, 6, 5, 4, 3, 2, 1, 0]
BF16 = jnp.bfloat16
F32 = jnp.float32


def halves(matrix):
    high = matrix.astype(np.float32).astype(ml_dtypes.bfloat16)
    low = (matrix - high.astype(np.float64)).astype(np.float32).astype(ml_dtypes.bfloat16)
    return np.concatenate([high, high, low], axis=0)


@functools.lru_cache(maxsize=1)
def tables():
    block = np.arange(BLOCKS)
    spot = np.arange(BLK)
    turn = np.exp(-2j * np.pi * np.outer(block + 0.25, spot) / POINTS)
    inner = np.exp(-2j * np.pi * np.outer(spot, spot) / BLK)
    forth = np.block([[inner.real, inner.imag], [-inner.imag, inner.real]])
    home = np.block([[inner.real, -inner.imag], [inner.imag, inner.real]]) / POINTS
    turns = np.stack([turn.real, turn.imag]).astype(np.float32)
    return turns, halves(forth), halves(home)


def plus(a, b):
    return a[0] + b[0], a[1] + b[1]


def minus(a, b):
    return a[0] - b[0], a[1] - b[1]


def times_i(a, sign):
    return (-a[1], a[0]) if sign > 0 else (a[1], -a[0])


def times(a, b):
    return a[0] * b[0] - a[1] * b[1], a[0] * b[1] + a[1] * b[0]


def rotated(a, angle):
    if angle == 0.0:
        return a
    return times(a, (math.cos(angle), math.sin(angle)))


def four(z, sign):
    even, odd = plus(z[0], z[2]), minus(z[0], z[2])
    both, turn = plus(z[1], z[3]), times_i(minus(z[1], z[3]), sign)
    return [plus(even, both), plus(odd, turn), minus(even, both), minus(odd, turn)]


def eight(z, sign):
    even, odd = four(z[0::2], sign), four(z[1::2], sign)
    root = math.sqrt(0.5)
    a, b, c, d = odd
    first = ((b[0] - sign * b[1]) * root, (b[1] + sign * b[0]) * root)
    third = ((-d[0] - sign * d[1]) * root, (sign * d[0] - d[1]) * root)
    odd = [a, first, times_i(c, sign), third]
    return [plus(e, o) for e, o in zip(even, odd)] + [minus(e, o) for e, o in zip(even, odd)]


def store_split(ref, base, at, value):
    for part in range(2):
        high = value[part].astype(BF16)
        low = (value[part] - high.astype(F32)).astype(BF16)
        ref[pl.ds(base + at * LANES, LANES), pl.ds(part * BLK, BLK)] = high
        ref[pl.ds(base + at * LANES, LANES), pl.ds((2 + part) * BLK, BLK)] = low


def load_pair(ref, base, at):
    rows = pl.ds(base + at * LANES, LANES)
    return ref[rows, pl.ds(0, BLK)], ref[rows, pl.ds(BLK, BLK)]


def forward_blocks(load, turn_ref, mid_ref, lhs_ref, base):
    for b in range(FAST):
        x = [load(b + FAST * a) for a in range(SLOW)]
        z = [(x[0], jnp.zeros_like(x[0]))]
        for a in range(1, SLOW):
            angle = -math.pi * a / 8
            z.append((x[a] * math.cos(angle), x[a] * math.sin(angle)))
        for p, value in enumerate(four(z, -1)):
            value = rotated(value, -2 * math.pi * b * (p + 0.25) / BLOCKS)
            mid_ref[b * SLOW + p, 0] = value[0]
            mid_ref[b * SLOW + p, 1] = value[1]
        yield
    for p in range(SLOW):
        z = [(mid_ref[b * SLOW + p, 0], mid_ref[b * SLOW + p, 1]) for b in range(FAST)]
        for q, value in enumerate(eight(z, -1)):
            k = p + SLOW * q
            value = times(value, (turn_ref[0, pl.ds(k, 1), :], turn_ref[1, pl.ds(k, 1), :]))
            store_split(lhs_ref, base, k, value)
        yield


def backward_blocks(store, turn_ref, mid_ref, wave_ref, base):
    for p in range(SLOW):
        z = []
        for q in range(FAST):
            k = p + SLOW * q
            turn = (turn_ref[0, pl.ds(k, 1), :], -turn_ref[1, pl.ds(k, 1), :])
            z.append(times(load_pair(wave_ref, base, k), turn))
        for b, value in enumerate(eight(z, 1)):
            value = rotated(value, 2 * math.pi * b * (p + 0.25) / BLOCKS)
            mid_ref[b * SLOW + p, 0] = value[0]
            mid_ref[b * SLOW + p, 1] = value[1]
        yield
    for b in range(FAST):
        z = [(mid_ref[b * SLOW + p, 0], mid_ref[b * SLOW + p, 1]) for p in range(SLOW)]
        for a, value in enumerate(four(z, 1)):
            angle = math.pi * a / 8
            real = value[0] if a == 0 else value[0] * math.cos(angle) - value[1] * math.sin(angle)
            store(b + FAST * a, real)
        yield


def lane_step(source, table, target, base):
    part = ROWS // SLOW
    for at in range(SLOW):
        rows = pl.ds(base + at * part, part)
        left = jnp.concatenate([source[rows, :], source[rows, pl.ds(0, 2 * BLK)]], axis=1)
        target[rows, :] = jnp.dot(left, table[...], preferred_element_type=F32)
        yield


def together(*pieces):
    total = max(count for _, count in pieces)
    done = [0] * len(pieces)
    for turn in range(1, total + 1):
        for i, (step, count) in enumerate(pieces):
            while done[i] * total < turn * count:
                next(step)
                done[i] += 1
    for step, _ in pieces:
        next(step, None)


def slots_of(order_ref, slot_ref):
    for k in range(BLOCKS):
        slot_ref[order_ref[RANKS[k]]] = k


def flip_kernel(in_ref, out_ref):
    out_ref[...] = in_ref[...].astype(F32).T.astype(BF16).reshape(BLOCKS, LANES, BLK)


def scale_kernel(x_ref, gain_ref, scaled_ref):
    scaled_ref[...] = (x_ref[...].astype(F32) * gain_ref[...]).T


def norm_kernel(width, scaled_ref, squares_ref, taps_ref, grad_ref, out_ref):
    inv_norm = lax.rsqrt(squares_ref[...] / width + EPS)
    normed = (scaled_ref[...] * inv_norm).astype(BF16)
    out_ref[:, :LANES, :] = taps_ref[...]
    out_ref[:, LANES : 2 * LANES, :] = grad_ref[...]
    out_ref[:, 2 * LANES :, :] = normed.reshape(BLOCKS, LANES, BLK)


def main_kernel(
    block_ref, lag_ref, all_ref, turn_ref, forth, home,
    out_ref,
    block_slot, lag_slot, mid_ref, lhs_ref, spec_ref, wave_ref,
):
    slots_of(block_ref, block_slot)
    slots_of(lag_ref, lag_slot)

    def load(slot, at):
        return lambda n: all_ref[slot[n], pl.ds(at * LANES, LANES), :].astype(F32)

    def store(slot, at):
        def one(n, value):
            out_ref[slot[n], pl.ds(at * LANES, LANES), :] = value.astype(BF16)

        return one

    loads = (load(lag_slot, 0), load(block_slot, 1), load(block_slot, 2))
    stores = (store(block_slot, 2), store(block_slot, 0), store(lag_slot, 1))

    def blocks_in(i):
        return forward_blocks(loads[i], turn_ref, mid_ref.at[i], lhs_ref, i * ROWS), FAST + SLOW

    def blocks_out(i):
        return backward_blocks(stores[i], turn_ref, mid_ref.at[i], wave_ref, i * ROWS), FAST + SLOW

    def lanes_in(i):
        return lane_step(lhs_ref, forth, spec_ref, i * ROWS), SLOW

    def lanes_out(i):
        return lane_step(lhs_ref, home, wave_ref, i * ROWS), SLOW

    def first_product():
        for k in range(BLOCKS):
            f, g = load_pair(spec_ref, 0, k), load_pair(spec_ref, ROWS, k)
            store_split(lhs_ref, 0, k, times((f[0], -f[1]), g))
            yield

    def other_products():
        for k in range(BLOCKS):
            f, g, s = (load_pair(spec_ref, i * ROWS, k) for i in range(3))
            store_split(lhs_ref, ROWS, k, times(f, s))
            store_split(lhs_ref, 2 * ROWS, k, times((s[0], -s[1]), g))
            yield

    together(blocks_in(0))
    together(lanes_in(0), blocks_in(1))
    together(lanes_in(1), blocks_in(2))
    together(lanes_in(2), (first_product(), BLOCKS))
    together(lanes_out(0), (other_products(), BLOCKS))
    together(lanes_out(1), blocks_out(0))
    together(lanes_out(2), blocks_out(1))
    together(blocks_out(2))


def finish_kernel(scale, in_ref, mixed_out, grad_out, taps_out, mixed_ref, grad_ref, taps_ref, sems):
    channels = BLOCKS * LANES

    def flip(at):
        part = in_ref[:, at * LANES : (at + 1) * LANES, :]
        return part.astype(F32).reshape(channels, BLK).T

    copies = [
        pltpu.make_async_copy(source, target, sems.at[i])
        for i, (source, target) in enumerate(
            ((taps_ref, taps_out), (mixed_ref, mixed_out), (grad_ref, grad_out))
        )
    ]
    taps_ref[...] = flip(1) * scale
    copies[0].start()
    mixed_ref[...] = flip(0).astype(BF16)
    copies[1].start()
    grad_ref[...] = flip(2).astype(BF16)
    copies[2].start()
    for copy in copies:
        copy.wait()


VMEM = pl.BlockSpec(memory_space=pltpu.VMEM)
SMEM = pl.BlockSpec(memory_space=pltpu.SMEM)
HBM = pl.BlockSpec(memory_space=pltpu.HBM)


def call(kernel, outs, specs, scratch=(), flops=0, moved=2**19, to=None):
    return pl.pallas_call(
        kernel,
        out_shape=outs,
        in_specs=specs,
        out_specs=jax.tree.map(lambda _: to or VMEM, outs),
        scratch_shapes=list(scratch),
        cost_estimate=pl.CostEstimate(flops=flops, bytes_accessed=moved, transcendentals=0),
        compiler_params=pltpu.CompilerParams(vmem_limit_bytes=24 * 2**20),
    )


def shaped(shape, dtype):
    return jax.ShapeDtypeStruct(shape, dtype)


def working():
    return [
        pltpu.SMEM((BLOCKS,), jnp.int32),
        pltpu.SMEM((BLOCKS,), jnp.int32),
        pltpu.VMEM((3, BLOCKS, 2, LANES, BLK), F32),
        pltpu.VMEM((3 * ROWS, 4 * BLK), BF16),
        pltpu.VMEM((3 * ROWS, 2 * BLK), F32),
        pltpu.VMEM((3 * ROWS, 2 * BLK), F32),
    ]


def per_device(activations, norm_gain, filter_taps, out_grad, block_order, lag_order):
    rows, channels = activations.shape
    width = channels * lax.axis_size("ch")
    exchange = functools.partial(
        lax.all_to_all,
        axis_name="ctx",
        split_axis=0,
        concat_axis=0,
        axis_index_groups=[RANKS],
        tiled=True,
    )
    values = activations.astype(F32)
    squares = jnp.sum(values * values, axis=1)
    block = shaped((BLOCKS, LANES, BLK), BF16)
    taps = call(flip_kernel, block, [VMEM])(filter_taps)
    grads = call(flip_kernel, block, [VMEM])(out_grad)
    scaled = call(scale_kernel, shaped((channels, rows), F32), [VMEM] * 2)(
        activations, norm_gain.reshape(1, channels)
    )
    for step in (2, 6, 1):
        if step == 1:
            squares, taps, grads, scaled = lax.optimization_barrier((squares, taps, grads, scaled))
        hop = [(i, i ^ step) for i in range(8)]
        squares = squares + lax.ppermute(squares, "ch", hop)
    normed = call(
        functools.partial(norm_kernel, width),
        shaped((BLOCKS, 3 * LANES, BLK), BF16),
        [VMEM] * 4,
    )(scaled, squares.reshape(1, rows), taps, grads)
    signal = exchange(normed)

    fixed = [jnp.asarray(t) for t in tables()]
    spec = shaped((ROWS, 2 * BLK), F32)
    out = call(
        main_kernel,
        shaped((BLOCKS, 3 * LANES, BLK), BF16),
        [SMEM] * 2 + [VMEM] * 4,
        working(),
        flops=2 * 10**9,
        moved=2 * 2**20,
    )(block_order, lag_order, signal, *fixed)
    out = exchange(out)
    results = (
        shaped((rows, channels), BF16),
        shaped((rows, channels), BF16),
        shaped((rows, channels), F32),
    )
    return call(
        functools.partial(finish_kernel, 1.0 / math.sqrt(POINTS)),
        results,
        [VMEM],
        [pltpu.VMEM(r.shape, r.dtype) for r in results] + [pltpu.SemaphoreType.DMA((3,))],
        to=HBM,
    )(out)


def solution(mesh):
    placed = (P("ctx", "ch"), P("ch"), P("ctx", "ch"), P("ctx", "ch"), P(), P())
    return jax.shard_map(
        per_device,
        mesh=mesh,
        in_specs=placed,
        out_specs=(P("ctx", "ch"), P("ctx", "ch"), P("ctx", "ch")),
        check_vma=False,
    )
```

```python
import functools
import math

import jax
import jax.numpy as jnp
import ml_dtypes
import numpy as np
from jax import lax
from jax.experimental import pallas as pl
from jax.experimental.pallas import tpu as pltpu
from jax.sharding import PartitionSpec as P

EPS = 1e-06
BLOCKS = 32
BLK = 128
LANES = 16
POINTS = BLOCKS * BLK
ROWS = BLOCKS * LANES
SLOW = 4
FAST = BLOCKS // SLOW
RANKS = [23, 22, 21, 20, 19, 18, 17, 16, 15, 14, 13, 12, 11, 10, 9, 8, 31, 30, 29, 28, 27, 26, 25, 24, 7, 6, 5, 4, 3, 2, 1, 0]
BF16 = jnp.bfloat16
F32 = jnp.float32


def halves(matrix):
    high = matrix.astype(np.float32).astype(ml_dtypes.bfloat16)
    low = (matrix - high.astype(np.float64)).astype(np.float32).astype(ml_dtypes.bfloat16)
    return np.concatenate([high, high, low], axis=0)


@functools.lru_cache(maxsize=1)
def tables():
    block = np.arange(BLOCKS)
    spot = np.arange(BLK)
    turn = np.exp(-2j * np.pi * np.outer(block + 0.25, spot) / POINTS)
    inner = np.exp(-2j * np.pi * np.outer(spot, spot) / BLK)
    forth = np.block([[inner.real, inner.imag], [-inner.imag, inner.real]])
    home = np.block([[inner.real, -inner.imag], [inner.imag, inner.real]]) / POINTS
    turns = np.stack([turn.real, turn.imag]).astype(np.float32)
    return turns, halves(forth), halves(home)


def plus(a, b):
    return a[0] + b[0], a[1] + b[1]


def minus(a, b):
    return a[0] - b[0], a[1] - b[1]


def times_i(a, sign):
    return (-a[1], a[0]) if sign > 0 else (a[1], -a[0])


def times(a, b):
    return a[0] * b[0] - a[1] * b[1], a[0] * b[1] + a[1] * b[0]


def rotated(a, angle):
    if angle == 0.0:
        return a
    return times(a, (math.cos(angle), math.sin(angle)))


def four(z, sign):
    even, odd = plus(z[0], z[2]), minus(z[0], z[2])
    both, turn = plus(z[1], z[3]), times_i(minus(z[1], z[3]), sign)
    return [plus(even, both), plus(odd, turn), minus(even, both), minus(odd, turn)]


def eight(z, sign):
    even, odd = four(z[0::2], sign), four(z[1::2], sign)
    root = math.sqrt(0.5)
    a, b, c, d = odd
    first = ((b[0] - sign * b[1]) * root, (b[1] + sign * b[0]) * root)
    third = ((-d[0] - sign * d[1]) * root, (sign * d[0] - d[1]) * root)
    odd = [a, first, times_i(c, sign), third]
    return [plus(e, o) for e, o in zip(even, odd)] + [minus(e, o) for e, o in zip(even, odd)]


def store_split(ref, base, at, value):
    for part in range(2):
        high = value[part].astype(BF16)
        low = (value[part] - high.astype(F32)).astype(BF16)
        ref[pl.ds(base + at * LANES, LANES), pl.ds(part * BLK, BLK)] = high
        ref[pl.ds(base + at * LANES, LANES), pl.ds((2 + part) * BLK, BLK)] = low


def load_pair(ref, base, at):
    rows = pl.ds(base + at * LANES, LANES)
    return ref[rows, pl.ds(0, BLK)], ref[rows, pl.ds(BLK, BLK)]


def forward_blocks(load, turn_ref, mid_ref, lhs_ref, base):
    for b in range(FAST):
        x = [load(b + FAST * a) for a in range(SLOW)]
        z = [(x[0], jnp.zeros_like(x[0]))]
        for a in range(1, SLOW):
            angle = -math.pi * a / 8
            z.append((x[a] * math.cos(angle), x[a] * math.sin(angle)))
        for p, value in enumerate(four(z, -1)):
            value = rotated(value, -2 * math.pi * b * (p + 0.25) / BLOCKS)
            mid_ref[b * SLOW + p, 0] = value[0]
            mid_ref[b * SLOW + p, 1] = value[1]
        yield
    for p in range(SLOW):
        z = [(mid_ref[b * SLOW + p, 0], mid_ref[b * SLOW + p, 1]) for b in range(FAST)]
        for q, value in enumerate(eight(z, -1)):
            k = p + SLOW * q
            value = times(value, (turn_ref[0, pl.ds(k, 1), :], turn_ref[1, pl.ds(k, 1), :]))
            store_split(lhs_ref, base, k, value)
        yield


def backward_blocks(store, turn_ref, mid_ref, wave_ref, base):
    for p in range(SLOW):
        z = []
        for q in range(FAST):
            k = p + SLOW * q
            turn = (turn_ref[0, pl.ds(k, 1), :], -turn_ref[1, pl.ds(k, 1), :])
            z.append(times(load_pair(wave_ref, base, k), turn))
        for b, value in enumerate(eight(z, 1)):
            value = rotated(value, 2 * math.pi * b * (p + 0.25) / BLOCKS)
            mid_ref[b * SLOW + p, 0] = value[0]
            mid_ref[b * SLOW + p, 1] = value[1]
        yield
    for b in range(FAST):
        z = [(mid_ref[b * SLOW + p, 0], mid_ref[b * SLOW + p, 1]) for p in range(SLOW)]
        for a, value in enumerate(four(z, 1)):
            angle = math.pi * a / 8
            real = value[0] if a == 0 else value[0] * math.cos(angle) - value[1] * math.sin(angle)
            store(b + FAST * a, real)
        yield


def lane_step(source, table, target, base):
    part = ROWS // SLOW
    for at in range(SLOW):
        rows = pl.ds(base + at * part, part)
        left = jnp.concatenate([source[rows, :], source[rows, pl.ds(0, 2 * BLK)]], axis=1)
        target[rows, :] = jnp.dot(left, table[...], preferred_element_type=F32)
        yield


def together(*pieces):
    total = max(count for _, count in pieces)
    done = [0] * len(pieces)
    for turn in range(1, total + 1):
        for i, (step, count) in enumerate(pieces):
            while done[i] * total < turn * count:
                next(step)
                done[i] += 1
    for step, _ in pieces:
        next(step, None)


def slots_of(order_ref, slot_ref):
    for k in range(BLOCKS):
        slot_ref[order_ref[RANKS[k]]] = k


def flip_kernel(in_ref, out_ref):
    out_ref[...] = in_ref[...].astype(F32).T.astype(BF16).reshape(BLOCKS, LANES, BLK)


def scale_kernel(x_ref, gain_ref, scaled_ref):
    scaled_ref[...] = (x_ref[...].astype(F32) * gain_ref[...]).T


def norm_kernel(width, scaled_ref, squares_ref, taps_ref, grad_ref, out_ref):
    inv_norm = lax.rsqrt(squares_ref[...] / width + EPS)
    normed = (scaled_ref[...] * inv_norm).astype(BF16)
    out_ref[:, :LANES, :] = taps_ref[...]
    out_ref[:, LANES : 2 * LANES, :] = grad_ref[...]
    out_ref[:, 2 * LANES :, :] = normed.reshape(BLOCKS, LANES, BLK)


def main_kernel(
    block_ref, lag_ref, all_ref, turn_ref, forth, home,
    out_ref,
    block_slot, lag_slot, mid_ref, lhs_ref, spec_ref, wave_ref,
):
    slots_of(block_ref, block_slot)
    slots_of(lag_ref, lag_slot)

    def load(slot, at):
        return lambda n: all_ref[slot[n], pl.ds(at * LANES, LANES), :].astype(F32)

    def store(slot, at):
        def one(n, value):
            out_ref[slot[n], pl.ds(at * LANES, LANES), :] = value.astype(BF16)

        return one

    loads = (load(lag_slot, 0), load(block_slot, 1), load(block_slot, 2))
    stores = (store(block_slot, 2), store(block_slot, 0), store(lag_slot, 1))

    def blocks_in(i):
        return forward_blocks(loads[i], turn_ref, mid_ref.at[i], lhs_ref, i * ROWS), FAST + SLOW

    def blocks_out(i):
        return backward_blocks(stores[i], turn_ref, mid_ref.at[i], wave_ref, i * ROWS), FAST + SLOW

    def lanes_in(i):
        return lane_step(lhs_ref, forth, spec_ref, i * ROWS), SLOW

    def lanes_out(i):
        return lane_step(lhs_ref, home, wave_ref, i * ROWS), SLOW

    def first_product():
        for k in range(BLOCKS):
            f, g = load_pair(spec_ref, 0, k), load_pair(spec_ref, ROWS, k)
            store_split(lhs_ref, 0, k, times((f[0], -f[1]), g))
            yield

    def other_products():
        for k in range(BLOCKS):
            f, g, s = (load_pair(spec_ref, i * ROWS, k) for i in range(3))
            store_split(lhs_ref, ROWS, k, times(f, s))
            store_split(lhs_ref, 2 * ROWS, k, times((s[0], -s[1]), g))
            yield

    together(blocks_in(0))
    together(lanes_in(0), blocks_in(1))
    together(lanes_in(1), blocks_in(2))
    together(lanes_in(2), (first_product(), BLOCKS))
    together(lanes_out(0), (other_products(), BLOCKS))
    together(lanes_out(1), blocks_out(0))
    together(lanes_out(2), blocks_out(1))
    together(blocks_out(2))


def finish_kernel(scale, in_ref, mixed_out, grad_out, taps_out, mixed_ref, grad_ref, taps_ref, sems):
    channels = BLOCKS * LANES

    def flip(at):
        part = in_ref[:, at * LANES : (at + 1) * LANES, :]
        return part.astype(F32).reshape(channels, BLK).T

    copies = [
        pltpu.make_async_copy(source, target, sems.at[i])
        for i, (source, target) in enumerate(
            ((taps_ref, taps_out), (mixed_ref, mixed_out), (grad_ref, grad_out))
        )
    ]
    taps_ref[...] = flip(1) * scale
    copies[0].start()
    mixed_ref[...] = flip(0).astype(BF16)
    copies[1].start()
    grad_ref[...] = flip(2).astype(BF16)
    copies[2].start()
    for copy in copies:
        copy.wait()


VMEM = pl.BlockSpec(memory_space=pltpu.VMEM)
SMEM = pl.BlockSpec(memory_space=pltpu.SMEM)
HBM = pl.BlockSpec(memory_space=pltpu.HBM)


def call(kernel, outs, specs, scratch=(), flops=0, moved=2**19, to=None):
    return pl.pallas_call(
        kernel,
        out_shape=outs,
        in_specs=specs,
        out_specs=jax.tree.map(lambda _: to or VMEM, outs),
        scratch_shapes=list(scratch),
        cost_estimate=pl.CostEstimate(flops=flops, bytes_accessed=moved, transcendentals=0),
        compiler_params=pltpu.CompilerParams(vmem_limit_bytes=24 * 2**20),
    )


def shaped(shape, dtype):
    return jax.ShapeDtypeStruct(shape, dtype)


def working():
    return [
        pltpu.SMEM((BLOCKS,), jnp.int32),
        pltpu.SMEM((BLOCKS,), jnp.int32),
        pltpu.VMEM((3, BLOCKS, 2, LANES, BLK), F32),
        pltpu.VMEM((3 * ROWS, 4 * BLK), BF16),
        pltpu.VMEM((3 * ROWS, 2 * BLK), F32),
        pltpu.VMEM((3 * ROWS, 2 * BLK), F32),
    ]


def per_device(activations, norm_gain, filter_taps, out_grad, block_order, lag_order):
    rows, channels = activations.shape
    width = channels * lax.axis_size("ch")
    exchange = functools.partial(
        lax.all_to_all,
        axis_name="ctx",
        split_axis=0,
        concat_axis=0,
        axis_index_groups=[RANKS],
        tiled=True,
    )
    values = activations.astype(F32)
    squares = jnp.sum(values * values, axis=1)
    block = shaped((BLOCKS, LANES, BLK), BF16)
    taps = call(flip_kernel, block, [VMEM])(filter_taps)
    grads = call(flip_kernel, block, [VMEM])(out_grad)
    scaled = call(scale_kernel, shaped((channels, rows), F32), [VMEM] * 2)(
        activations, norm_gain.reshape(1, channels)
    )
    others = [
        lax.ppermute(squares, "ch", [(i, (i + step) % 8) for i in range(8)]) for step in (2, 4, 6)
    ]
    squares = squares + others[0] + others[1] + others[2]
    squares, taps, grads, scaled = lax.optimization_barrier((squares, taps, grads, scaled))
    squares = squares + lax.ppermute(squares, "ch", [(i, i ^ 1) for i in range(8)])
    normed = call(
        functools.partial(norm_kernel, width),
        shaped((BLOCKS, 3 * LANES, BLK), BF16),
        [VMEM] * 4,
    )(scaled, squares.reshape(1, rows), taps, grads)
    signal = exchange(normed)

    fixed = [jnp.asarray(t) for t in tables()]
    spec = shaped((ROWS, 2 * BLK), F32)
    out = call(
        main_kernel,
        shaped((BLOCKS, 3 * LANES, BLK), BF16),
        [SMEM] * 2 + [VMEM] * 4,
        working(),
        flops=2 * 10**9,
        moved=2 * 2**20,
    )(block_order, lag_order, signal, *fixed)
    out = exchange(out)
    results = (
        shaped((rows, channels), BF16),
        shaped((rows, channels), BF16),
        shaped((rows, channels), F32),
    )
    return call(
        functools.partial(finish_kernel, 1.0 / math.sqrt(POINTS)),
        results,
        [VMEM],
        [pltpu.VMEM(r.shape, r.dtype) for r in results] + [pltpu.SemaphoreType.DMA((3,))],
        to=HBM,
    )(out)


def solution(mesh):
    placed = (P("ctx", "ch"), P("ch"), P("ctx", "ch"), P("ctx", "ch"), P(), P())
    return jax.shard_map(
        per_device,
        mesh=mesh,
        in_specs=placed,
        out_specs=(P("ctx", "ch"), P("ctx", "ch"), P("ctx", "ch")),
        check_vma=False,
    )
```

```python
import functools
import math

import jax
import jax.numpy as jnp
import ml_dtypes
import numpy as np
from jax import lax
from jax.experimental import pallas as pl
from jax.experimental.pallas import tpu as pltpu
from jax.sharding import PartitionSpec as P

EPS = 1e-06
BLOCKS = 32
BLK = 128
LANES = 16
POINTS = BLOCKS * BLK
ROWS = BLOCKS * LANES
SLOW = 4
FAST = BLOCKS // SLOW
RANKS = [21, 20, 23, 22, 19, 18, 17, 16, 13, 12, 15, 14, 11, 10, 9, 8, 29, 28, 31, 30, 27, 26, 25, 24, 5, 4, 7, 6, 3, 2, 1, 0]
BF16 = jnp.bfloat16
F32 = jnp.float32


def halves(matrix):
    high = matrix.astype(np.float32).astype(ml_dtypes.bfloat16)
    low = (matrix - high.astype(np.float64)).astype(np.float32).astype(ml_dtypes.bfloat16)
    return np.concatenate([high, high, low], axis=0)


@functools.lru_cache(maxsize=1)
def tables():
    block = np.arange(BLOCKS)
    spot = np.arange(BLK)
    turn = np.exp(-2j * np.pi * np.outer(block + 0.25, spot) / POINTS)
    inner = np.exp(-2j * np.pi * np.outer(spot, spot) / BLK)
    forth = np.block([[inner.real, inner.imag], [-inner.imag, inner.real]])
    home = np.block([[inner.real, -inner.imag], [inner.imag, inner.real]]) / POINTS
    turns = np.stack([turn.real, turn.imag]).astype(np.float32)
    return turns, halves(forth), halves(home)


def plus(a, b):
    return a[0] + b[0], a[1] + b[1]


def minus(a, b):
    return a[0] - b[0], a[1] - b[1]


def times_i(a, sign):
    return (-a[1], a[0]) if sign > 0 else (a[1], -a[0])


def times(a, b):
    return a[0] * b[0] - a[1] * b[1], a[0] * b[1] + a[1] * b[0]


def rotated(a, angle):
    if angle == 0.0:
        return a
    return times(a, (math.cos(angle), math.sin(angle)))


def four(z, sign):
    even, odd = plus(z[0], z[2]), minus(z[0], z[2])
    both, turn = plus(z[1], z[3]), times_i(minus(z[1], z[3]), sign)
    return [plus(even, both), plus(odd, turn), minus(even, both), minus(odd, turn)]


def eight(z, sign):
    even, odd = four(z[0::2], sign), four(z[1::2], sign)
    root = math.sqrt(0.5)
    a, b, c, d = odd
    first = ((b[0] - sign * b[1]) * root, (b[1] + sign * b[0]) * root)
    third = ((-d[0] - sign * d[1]) * root, (sign * d[0] - d[1]) * root)
    odd = [a, first, times_i(c, sign), third]
    return [plus(e, o) for e, o in zip(even, odd)] + [minus(e, o) for e, o in zip(even, odd)]


def store_split(ref, base, at, value):
    for part in range(2):
        high = value[part].astype(BF16)
        low = (value[part] - high.astype(F32)).astype(BF16)
        ref[pl.ds(base + at * LANES, LANES), pl.ds(part * BLK, BLK)] = high
        ref[pl.ds(base + at * LANES, LANES), pl.ds((2 + part) * BLK, BLK)] = low


def load_pair(ref, base, at):
    rows = pl.ds(base + at * LANES, LANES)
    return ref[rows, pl.ds(0, BLK)], ref[rows, pl.ds(BLK, BLK)]


def forward_blocks(load, turn_ref, mid_ref, lhs_ref, base):
    for b in range(FAST):
        x = [load(b + FAST * a) for a in range(SLOW)]
        z = [(x[0], jnp.zeros_like(x[0]))]
        for a in range(1, SLOW):
            angle = -math.pi * a / 8
            z.append((x[a] * math.cos(angle), x[a] * math.sin(angle)))
        for p, value in enumerate(four(z, -1)):
            value = rotated(value, -2 * math.pi * b * (p + 0.25) / BLOCKS)
            mid_ref[b * SLOW + p, 0] = value[0]
            mid_ref[b * SLOW + p, 1] = value[1]
        yield
    for p in range(SLOW):
        z = [(mid_ref[b * SLOW + p, 0], mid_ref[b * SLOW + p, 1]) for b in range(FAST)]
        for q, value in enumerate(eight(z, -1)):
            k = p + SLOW * q
            value = times(value, (turn_ref[0, pl.ds(k, 1), :], turn_ref[1, pl.ds(k, 1), :]))
            store_split(lhs_ref, base, k, value)
        yield


def backward_blocks(store, turn_ref, mid_ref, wave_ref, base):
    for p in range(SLOW):
        z = []
        for q in range(FAST):
            k = p + SLOW * q
            turn = (turn_ref[0, pl.ds(k, 1), :], -turn_ref[1, pl.ds(k, 1), :])
            z.append(times(load_pair(wave_ref, base, k), turn))
        for b, value in enumerate(eight(z, 1)):
            value = rotated(value, 2 * math.pi * b * (p + 0.25) / BLOCKS)
            mid_ref[b * SLOW + p, 0] = value[0]
            mid_ref[b * SLOW + p, 1] = value[1]
        yield
    for b in range(FAST):
        z = [(mid_ref[b * SLOW + p, 0], mid_ref[b * SLOW + p, 1]) for p in range(SLOW)]
        for a, value in enumerate(four(z, 1)):
            angle = math.pi * a / 8
            real = value[0] if a == 0 else value[0] * math.cos(angle) - value[1] * math.sin(angle)
            store(b + FAST * a, real)
        yield


def lane_step(source, table, target, base):
    part = ROWS // SLOW
    for at in range(SLOW):
        rows = pl.ds(base + at * part, part)
        left = jnp.concatenate([source[rows, :], source[rows, pl.ds(0, 2 * BLK)]], axis=1)
        target[rows, :] = jnp.dot(left, table[...], preferred_element_type=F32)
        yield


def together(*pieces):
    total = max(count for _, count in pieces)
    done = [0] * len(pieces)
    for turn in range(1, total + 1):
        for i, (step, count) in enumerate(pieces):
            while done[i] * total < turn * count:
                next(step)
                done[i] += 1
    for step, _ in pieces:
        next(step, None)


def slots_of(order_ref, slot_ref):
    for k in range(BLOCKS):
        slot_ref[order_ref[RANKS[k]]] = k


def flip_kernel(in_ref, out_ref):
    out_ref[...] = in_ref[...].astype(F32).T.astype(BF16).reshape(BLOCKS, LANES, BLK)


def scale_kernel(x_ref, gain_ref, scaled_ref):
    scaled_ref[...] = (x_ref[...].astype(F32) * gain_ref[...]).T


def norm_kernel(width, scaled_ref, squares_ref, taps_ref, grad_ref, out_ref):
    inv_norm = lax.rsqrt(squares_ref[...] / width + EPS)
    normed = (scaled_ref[...] * inv_norm).astype(BF16)
    out_ref[:, :LANES, :] = taps_ref[...]
    out_ref[:, LANES : 2 * LANES, :] = grad_ref[...]
    out_ref[:, 2 * LANES :, :] = normed.reshape(BLOCKS, LANES, BLK)


def main_kernel(
    block_ref, lag_ref, all_ref, turn_ref, forth, home,
    out_ref,
    block_slot, lag_slot, mid_ref, lhs_ref, spec_ref, wave_ref,
):
    slots_of(block_ref, block_slot)
    slots_of(lag_ref, lag_slot)

    def load(slot, at):
        return lambda n: all_ref[slot[n], pl.ds(at * LANES, LANES), :].astype(F32)

    def store(slot, at):
        def one(n, value):
            out_ref[slot[n], pl.ds(at * LANES, LANES), :] = value.astype(BF16)

        return one

    loads = (load(lag_slot, 0), load(block_slot, 1), load(block_slot, 2))
    stores = (store(block_slot, 2), store(block_slot, 0), store(lag_slot, 1))

    def blocks_in(i):
        return forward_blocks(loads[i], turn_ref, mid_ref.at[i], lhs_ref, i * ROWS), FAST + SLOW

    def blocks_out(i):
        return backward_blocks(stores[i], turn_ref, mid_ref.at[i], wave_ref, i * ROWS), FAST + SLOW

    def lanes_in(i):
        return lane_step(lhs_ref, forth, spec_ref, i * ROWS), SLOW

    def lanes_out(i):
        return lane_step(lhs_ref, home, wave_ref, i * ROWS), SLOW

    def first_product():
        for k in range(BLOCKS):
            f, g = load_pair(spec_ref, 0, k), load_pair(spec_ref, ROWS, k)
            store_split(lhs_ref, 0, k, times((f[0], -f[1]), g))
            yield

    def other_products():
        for k in range(BLOCKS):
            f, g, s = (load_pair(spec_ref, i * ROWS, k) for i in range(3))
            store_split(lhs_ref, ROWS, k, times(f, s))
            store_split(lhs_ref, 2 * ROWS, k, times((s[0], -s[1]), g))
            yield

    together(blocks_in(0))
    together(lanes_in(0), blocks_in(1))
    together(lanes_in(1), blocks_in(2))
    together(lanes_in(2), (first_product(), BLOCKS))
    together(lanes_out(0), (other_products(), BLOCKS))
    together(lanes_out(1), blocks_out(0))
    together(lanes_out(2), blocks_out(1))
    together(blocks_out(2))


def finish_kernel(scale, in_ref, mixed_out, grad_out, taps_out, mixed_ref, grad_ref, taps_ref, sems):
    channels = BLOCKS * LANES

    def flip(at):
        part = in_ref[:, at * LANES : (at + 1) * LANES, :]
        return part.astype(F32).reshape(channels, BLK).T

    copies = [
        pltpu.make_async_copy(source, target, sems.at[i])
        for i, (source, target) in enumerate(
            ((taps_ref, taps_out), (mixed_ref, mixed_out), (grad_ref, grad_out))
        )
    ]
    taps_ref[...] = flip(1) * scale
    copies[0].start()
    mixed_ref[...] = flip(0).astype(BF16)
    copies[1].start()
    grad_ref[...] = flip(2).astype(BF16)
    copies[2].start()
    for copy in copies:
        copy.wait()


VMEM = pl.BlockSpec(memory_space=pltpu.VMEM)
SMEM = pl.BlockSpec(memory_space=pltpu.SMEM)
HBM = pl.BlockSpec(memory_space=pltpu.HBM)


def call(kernel, outs, specs, scratch=(), flops=0, moved=2**19, to=None):
    return pl.pallas_call(
        kernel,
        out_shape=outs,
        in_specs=specs,
        out_specs=jax.tree.map(lambda _: to or VMEM, outs),
        scratch_shapes=list(scratch),
        cost_estimate=pl.CostEstimate(flops=flops, bytes_accessed=moved, transcendentals=0),
        compiler_params=pltpu.CompilerParams(vmem_limit_bytes=24 * 2**20),
    )


def shaped(shape, dtype):
    return jax.ShapeDtypeStruct(shape, dtype)


def working():
    return [
        pltpu.SMEM((BLOCKS,), jnp.int32),
        pltpu.SMEM((BLOCKS,), jnp.int32),
        pltpu.VMEM((3, BLOCKS, 2, LANES, BLK), F32),
        pltpu.VMEM((3 * ROWS, 4 * BLK), BF16),
        pltpu.VMEM((3 * ROWS, 2 * BLK), F32),
        pltpu.VMEM((3 * ROWS, 2 * BLK), F32),
    ]


def per_device(activations, norm_gain, filter_taps, out_grad, block_order, lag_order):
    rows, channels = activations.shape
    width = channels * lax.axis_size("ch")
    exchange = functools.partial(
        lax.all_to_all,
        axis_name="ctx",
        split_axis=0,
        concat_axis=0,
        axis_index_groups=[RANKS],
        tiled=True,
    )
    values = activations.astype(F32)
    squares = jnp.sum(values * values, axis=1)
    block = shaped((BLOCKS, LANES, BLK), BF16)
    taps = call(flip_kernel, block, [VMEM])(filter_taps)
    grads = call(flip_kernel, block, [VMEM])(out_grad)
    scaled = call(scale_kernel, shaped((channels, rows), F32), [VMEM] * 2)(
        activations, norm_gain.reshape(1, channels)
    )
    for step in (2, 6, 1):
        if step == 1:
            squares, taps, grads, scaled = lax.optimization_barrier((squares, taps, grads, scaled))
        hop = [(i, i ^ step) for i in range(8)]
        squares = squares + lax.ppermute(squares, "ch", hop)
    normed = call(
        functools.partial(norm_kernel, width),
        shaped((BLOCKS, 3 * LANES, BLK), BF16),
        [VMEM] * 4,
    )(scaled, squares.reshape(1, rows), taps, grads)
    signal = exchange(normed)

    fixed = [jnp.asarray(t) for t in tables()]
    spec = shaped((ROWS, 2 * BLK), F32)
    out = call(
        main_kernel,
        shaped((BLOCKS, 3 * LANES, BLK), BF16),
        [SMEM] * 2 + [VMEM] * 4,
        working(),
        flops=2 * 10**9,
        moved=2 * 2**20,
    )(block_order, lag_order, signal, *fixed)
    out = exchange(out)
    results = (
        shaped((rows, channels), BF16),
        shaped((rows, channels), BF16),
        shaped((rows, channels), F32),
    )
    return call(
        functools.partial(finish_kernel, 1.0 / math.sqrt(POINTS)),
        results,
        [VMEM],
        [pltpu.VMEM(r.shape, r.dtype) for r in results] + [pltpu.SemaphoreType.DMA((3,))],
        to=HBM,
    )(out)


def solution(mesh):
    placed = (P("ctx", "ch"), P("ch"), P("ctx", "ch"), P("ctx", "ch"), P(), P())
    return jax.shard_map(
        per_device,
        mesh=mesh,
        in_specs=placed,
        out_specs=(P("ctx", "ch"), P("ctx", "ch"), P("ctx", "ch")),
        check_vma=False,
    )
```
